768 devices in a mesh: row: 24 (over x_hi, z), col: 32 (over y, x_lo, core).
Axes of the slice: x: 4 (x_hi: 2, x_lo: 2; x = x_hi * 2 + x_lo), y: 8, z: 12, core: 2. Of those that a mesh axis runs over, the one named last changes fastest.
Arguments:
- amplitudes: bfloat16 [2, 4608, 16384], P(None, 'row', 'col'), may hold values from -6 to 6
- integrals: bfloat16 [2, 16384, 6144], P(None, 'col', 'row'), may hold values from -0.03125 to 0.03125
- amp_mask: int32 [2, 72, 256], P(None, 'row', 'col'), may hold values 0 or 1
- int_mask: int32 [2, 256, 96], P(None, 'col', 'row'), may hold values 0 or 1
- owners: int32 [72], replicated, may hold values from 0 to 31, as said below
Outputs:
- residual_tiles: float32 [32, 3, 64, 6144], P('col', None, None, 'row')
The draws below stay inside these ranges and needn't reach their ends.
Inputs may be any that keep to these rules, and one draw needn't show every extreme that they name: `owners`: each index of col owns at most 3 tiles, and some index owns exactly 3; indices 0 and 31 own at least one tile.
All inputs are finite; a program needn't handle non-finite values. No bound on the sum of `amp_mask` or of `int_mask` on one device may be relied on, other than what follows from the above.
Results may differ from the reference program's by a relative error of at most 0.015.
Values may be sent and summed in bfloat16 or wider, within the bound.
No kernel may reach another device: no remote copies, remote signals or barrier semaphores. Data moves between devices by JAX's collectives and lax.ppermute only.
A program may use at most 64 MiB of HBM per device.

```python
import jax
import jax.numpy as jnp
from jax import lax

TILE = 64
KT = 8
NT = 4
STEPS = 2
MT = 72
CAP = 3
KW = 512
MROWS = 4608
KTOT = 16384
NTOT = 6144
N_ROW = 24
N_COL = 32


def draw_owners(key, part):
    key = jax.random.fold_in(key, 11)
    first_key, second_key, third_key = jax.random.split(key, 3)
    slot_total = N_COL * CAP
    positions = jnp.arange(slot_total, dtype=jnp.int32)
    slot_owner = positions // CAP
    special = jax.random.randint(first_key, (), 0, N_COL, dtype=jnp.int32)
    priority = jax.random.permutation(second_key, slot_total).astype(jnp.int32)
    forced = (slot_owner == special) | (positions == 0) | (positions == slot_total - CAP)
    priority = jnp.where(forced, positions - 2 * slot_total, priority)
    ordering = jnp.argsort(priority, stable=True)
    chosen = slot_owner[ordering[:MT]]
    shuffle = jax.random.permutation(third_key, MT)
    return chosen[shuffle].astype(jnp.int32)


def with_ends(values, stream_key, least, high):
    extent = values.shape
    index_at = [jax.random.randint(jax.random.fold_in(stream_key, axis), (), 0, extent[axis]) for axis in range(len(extent))]
    values = values.at[tuple(index_at)].set(least)
    longest = extent.index(max(extent))
    index_at[longest] = (index_at[longest] + 1) % extent[longest]
    return values.at[tuple(index_at)].set(high)


def block_levels(key, dims, shards, low, top_value):
    factor_of, own = 1.0, jax.random.fold_in(key, 6)
    for position, shards_of in shards:
        draws = jnp.exp(jax.random.uniform(jax.random.fold_in(own, position), (shards_of,), jnp.float32, low / len(shards), top_value / len(shards)))
        factor_of = factor_of * jnp.repeat(draws, dims[position] // shards_of).reshape([-1 if axis == position else 1 for axis in range(len(dims))])
    return factor_of


def gaussian(own_key, dims, spread, most, pieces=(), kind=jnp.bfloat16):
    factor_of = block_levels(own_key, dims, pieces, -0.22, 0.18) if pieces else 1.0
    entries = jax.random.normal(own_key, dims, jnp.float32) * spread * factor_of
    return jnp.minimum(jnp.maximum(entries, -most), most).astype(kind)


def setup_inputs(seed: int = 0) -> dict:
    seeds = jax.random.split(jax.random.key(seed), 6)
    amplitudes = gaussian(seeds[0], (STEPS, MROWS, KTOT), 1.0, 6.0, ((1, 24), (2, 32)))
    integrals = gaussian(seeds[1], (STEPS, KTOT, NTOT), (STEPS * KTOT) ** -0.5, 0.03125, ((1, 32), (2, 24)))
    amp_mask = with_ends((jax.random.randint(seeds[2], (STEPS, MT, KT * N_COL), 0, 4) < 3).astype(jnp.int32), jax.random.fold_in(seeds[2], 1), 0, 1)
    int_mask = with_ends((jax.random.randint(seeds[3], (STEPS, KT * N_COL, NT * N_ROW), 0, 4) < 3).astype(jnp.int32), jax.random.fold_in(seeds[3], 1), 0, 1)
    owners = draw_owners(jax.random.fold_in(seeds[5], 71), 0)
    return {"amplitudes": amplitudes, "integrals": integrals, "amp_mask": amp_mask, "int_mask": int_mask, "owners": owners}


def expand(mask, dtype):
    grown = jnp.repeat(jnp.repeat(mask, TILE, axis=-2), TILE, axis=-1)
    return grown.astype(dtype)


def reference(amplitudes, integrals, amp_mask, int_mask, owners):
    amp_used = amplitudes * expand(amp_mask, amplitudes.dtype)
    int_used = integrals * expand(int_mask, integrals.dtype)

    def accumulate(running, column_index):
        begin = (column_index * KW).astype(jnp.int32)
        amp_block = lax.dynamic_slice_in_dim(amp_used, begin, KW, 2)
        int_block = lax.dynamic_slice_in_dim(int_used, begin, KW, 1)
        partial_value = jnp.zeros((MROWS, NTOT), jnp.float32)
        for panel_index in range(STEPS):
            partial_value = partial_value + jnp.dot(amp_block[panel_index], int_block[panel_index], preferred_element_type=jnp.float32)
        rounded = lax.optimization_barrier(partial_value.astype(jnp.bfloat16))
        return running + rounded.astype(jnp.float32), None

    ladder, _ = lax.scan(accumulate, jnp.zeros((MROWS, NTOT), jnp.float32), jnp.arange(N_COL, dtype=jnp.int32))
    positions = jnp.arange(MT, dtype=jnp.int32)
    same_owner = owners[:, None] == owners[None, :]
    earlier = positions[:, None] > positions[None, :]
    slot_index = jnp.sum((same_owner & earlier).astype(jnp.int32), axis=1).astype(jnp.int32)
    tile_rows = ladder.reshape(MT, TILE, NTOT)
    result = jnp.zeros((N_COL, CAP, TILE, NTOT), jnp.float32)
    return result.at[owners, slot_index].set(tile_rows)
```

```python
import jax
import jax.numpy as jnp
from jax import lax
from jax.sharding import Mesh, PartitionSpec as P

SIZES = {"xh": 2, "z": 12, "y": 8, "xl": 2, "core": 2}
GROUP = ("xh", "xl", "core")
EDGE = 64
CAP = 3
PARTS = 8
PART_ROWS = EDGE // PARTS
SWAP = [(0, 1), (1, 0)]


def expand(mask, dtype):
    grown = jnp.repeat(jnp.repeat(mask, EDGE, axis=-2), EDGE, axis=-1)
    return grown.astype(dtype)


def pair(value, axis, dim):
    other = lax.ppermute(value, axis, SWAP)
    first = lax.axis_index(axis) == 0
    low = jnp.where(first, value, other)
    high = jnp.where(first, other, value)
    return jnp.concatenate([low, high], axis=dim)


def body(amplitudes, integrals, amp_mask, int_mask, owners):
    panels, rows, depth = amplitudes.shape
    local_tiles = rows // EDGE
    width = integrals.shape[2]
    tile_total = owners.shape[0]
    col_count = SIZES["y"] * SIZES["xl"] * SIZES["core"]

    amp_used = amplitudes * expand(amp_mask, amplitudes.dtype)
    parts = amp_used.reshape(panels, local_tiles, PARTS, PART_ROWS, depth)
    parts = parts.transpose(2, 0, 1, 3, 4).reshape(PARTS, panels * local_tiles * PART_ROWS, depth)
    traded = lax.all_to_all(parts, GROUP, split_axis=0, concat_axis=0, tiled=True)
    traded = traded.reshape(2, 4, panels, local_tiles * PART_ROWS, depth)
    traded = traded.transpose(0, 3, 1, 2, 4).reshape(2 * local_tiles * PART_ROWS, 4 * panels * depth)
    left = lax.all_gather(traded, "z", axis=0, tiled=True)

    int_used = integrals * expand(int_mask, integrals.dtype)
    right = pair(int_used, "xh", 2)
    right = pair(right[None], "xl", 0)
    right = pair(right[:, None], "core", 1)
    right = right.reshape(4 * panels * depth, 2 * width)

    partial_value = jnp.dot(left, right, preferred_element_type=jnp.float32).astype(jnp.bfloat16)

    positions = jnp.arange(tile_total, dtype=jnp.int32)
    same_owner = owners[:, None] == owners[None, :]
    earlier = positions[:, None] > positions[None, :]
    slot_index = jnp.sum((same_owner & earlier).astype(jnp.int32), axis=1)
    destination = owners * CAP + slot_index
    held = destination.reshape(2, SIZES["z"], local_tiles).transpose(1, 0, 2).reshape(tile_total)
    source_row = (held[:, None] * PART_ROWS + jnp.arange(PART_ROWS, dtype=jnp.int32)).reshape(-1)
    slot_rows = jnp.arange(col_count * CAP * PART_ROWS, dtype=jnp.int32)
    selector = (slot_rows[:, None] == source_row[None, :]).astype(jnp.bfloat16)
    slots = jnp.dot(selector, partial_value, preferred_element_type=jnp.float32).astype(jnp.bfloat16)

    send = slots.reshape(SIZES["y"], 4 * CAP * PART_ROWS, 2 * width)
    received = lax.all_to_all(send, "y", split_axis=0, concat_axis=0, tiled=True)
    summed = jnp.sum(received.astype(jnp.float32), axis=0)
    summed = summed.reshape(4, CAP * PART_ROWS, 2, width).transpose(2, 0, 1, 3)
    summed = summed.reshape(PARTS, CAP * PART_ROWS, width)
    gathered = lax.all_to_all(summed, GROUP, split_axis=0, concat_axis=0, tiled=True)
    gathered = gathered.reshape(PARTS, CAP, PART_ROWS, width).transpose(1, 0, 2, 3)
    return gathered.reshape(1, CAP, EDGE, width)


def solution(mesh):
    fine = Mesh(mesh.devices.reshape(tuple(SIZES.values())), tuple(SIZES))
    row, col = ("xh", "z"), ("y", "xl", "core")
    in_specs = (
        P(None, row, col),
        P(None, col, row),
        P(None, row, col),
        P(None, col, row),
        P(),
    )
    out_specs = P(col, None, None, row)
    return jax.shard_map(body, mesh=fine, in_specs=in_specs, out_specs=out_specs, check_vma=False)
```

```python
import jax
import jax.numpy as jnp
from jax import lax
from jax.experimental import pallas as pl
from jax.experimental.pallas import tpu as pltpu
from jax.sharding import Mesh, PartitionSpec as P

SIZES = {"xh": 2, "z": 12, "yq": 4, "yb": 2, "xl": 2, "core": 2}
GROUP = ("xh", "yb", "xl", "core")
OWNERS = ("xh", "yq", "yb", "xl", "core")
RING = ("xh", "xl")
EDGE = 64
CAP = 3
LANES = 128
PARTS = 16
PART_ROWS = EDGE // PARTS
SLICES = 8
SWAP = [(0, 1), (1, 0)]
MIB = 1 << 20


def expand(mask, dtype):
    grown = jnp.repeat(jnp.repeat(mask, EDGE, axis=-2), EDGE, axis=-1)
    return grown.astype(dtype)


def turn(value, step):
    return lax.ppermute(value, RING, [(i, (i + step) % 4) for i in range(4)])


def contract(place_ref, left_ref, select_ref, *rest):
    pieces, (out_ref, slab_ref, total_ref, sems) = rest[:-4], rest[-4:]
    depth, width = pieces[0].shape
    copies = []
    for number in range(SLICES):
        begin = pl.multiple_of(place_ref[number, 0] * depth, depth)
        copy = pltpu.make_async_copy(
            left_ref.at[:, pl.ds(begin, depth)], slab_ref.at[number], sems.at[number]
        )
        copy.start()
        copies.append(copy)
    for number in range(SLICES):
        copies[number].wait()
        for side in range(2):
            term = jnp.dot(
                slab_ref[number], pieces[2 * number + side][...], preferred_element_type=jnp.float32
            )
            half = place_ref[number, 1 + side]
            if number == 0:
                total_ref[half] = term
            else:
                total_ref[half] += term
    rows = select_ref.shape[0]
    for half in range(2):
        rounded = total_ref[half].astype(jnp.bfloat16)
        stacked = jnp.concatenate([rounded[:, :LANES], rounded[:, LANES:]], axis=0)
        placed = jnp.dot(select_ref[...], stacked, preferred_element_type=jnp.float32)
        out_ref[half * rows:(half + 1) * rows, :] = placed.astype(jnp.bfloat16)


def body(amplitudes, integrals, amp_mask, int_mask, owners):
    panels, rows, depth = amplitudes.shape
    local_tiles = rows // EDGE
    width = integrals.shape[2]
    tile_total = owners.shape[0]
    slot_total = SIZES["yq"] * SLICES * CAP
    xh, yb, xl, core = (lax.axis_index(name) for name in GROUP)

    int_used = integrals * expand(int_mask, integrals.dtype)
    own = int_used.reshape(panels * depth, width)
    across = lax.ppermute(own, "yb", SWAP)
    low = [turn(own, 1), turn(across, 1)]
    high = [turn(own, -1), turn(across, -1)]
    far = [turn(low[0], 1), turn(high[1], -1)]
    here = []
    for near, beyond in (((own, across), far), (low, high)):
        for side in range(2):
            here += [near[side], beyond[side]]
    there = [lax.ppermute(value, "core", SWAP) for value in here]
    chip = xh * 2 + xl
    place = []
    for core_at in (core, 1 - core):
        for first, second in ((0, 2), (3, 1)):
            for side in (yb, 1 - yb):
                one, other = (chip + first) % 4, (chip + second) % 4
                place.append(jnp.stack([side * 4 + (one % 2) * 2 + core_at, one // 2, other // 2]))
    place = jnp.stack(place).astype(jnp.int32)

    amp_used = amplitudes * expand(amp_mask, amplitudes.dtype)
    parts = amp_used.reshape(panels, local_tiles, PARTS, PART_ROWS, depth)
    parts = parts.transpose(2, 0, 1, 3, 4).reshape(PARTS, panels * local_tiles * PART_ROWS, depth)
    traded = lax.all_to_all(parts, GROUP, split_axis=0, concat_axis=0, tiled=True)
    traded = traded.reshape(2, SLICES, panels, local_tiles * PART_ROWS, depth)
    traded = traded.transpose(0, 3, 1, 2, 4).reshape(2 * local_tiles * PART_ROWS, SLICES * panels * depth)
    left = lax.all_gather(traded, "z", axis=0, tiled=True)

    positions = jnp.arange(tile_total, dtype=jnp.int32)
    same_owner = owners[:, None] == owners[None, :]
    earlier = positions[:, None] > positions[None, :]
    slot_index = jnp.sum((same_owner & earlier).astype(jnp.int32), axis=1)
    destination = owners * CAP + slot_index
    held = destination.reshape(2, SIZES["z"], local_tiles).transpose(1, 0, 2).reshape(tile_total)
    source_row = (held[:, None] * PART_ROWS + jnp.arange(PART_ROWS, dtype=jnp.int32)).reshape(-1)
    owner_rows = CAP * PART_ROWS
    source_row = source_row // owner_rows * (2 * owner_rows) + source_row % owner_rows
    source_row = jnp.concatenate([source_row, source_row + owner_rows])
    slot_rows = jnp.arange(2 * slot_total * PART_ROWS, dtype=jnp.int32)
    selector = (slot_rows[:, None] == source_row[None, :]).astype(jnp.bfloat16)

    vmem = pl.BlockSpec(memory_space=pltpu.VMEM)
    slots = pl.pallas_call(
        contract,
        out_shape=jax.ShapeDtypeStruct((2 * selector.shape[0], LANES), jnp.bfloat16),
        in_specs=[pl.BlockSpec(memory_space=pltpu.SMEM), pl.BlockSpec(memory_space=pl.ANY)] + [vmem] * 17,
        out_specs=vmem,
        scratch_shapes=[
            pltpu.VMEM((SLICES, left.shape[0], panels * depth), jnp.bfloat16),
            pltpu.VMEM((2, left.shape[0], width), jnp.float32),
            pltpu.SemaphoreType.DMA((SLICES,)),
        ],
        compiler_params=pltpu.CompilerParams(vmem_limit_bytes=40 * MIB),
        cost_estimate=pl.CostEstimate(
            flops=2 * left.size * 2 * width, bytes_accessed=4 * left.size, transcendentals=0
        ),
    )(place, left, selector, *here, *there)

    received = lax.all_to_all(slots, OWNERS, split_axis=0, concat_axis=0, tiled=True)
    received = received.reshape(2, SIZES["yq"], SLICES, 2, CAP, PART_ROWS, LANES).astype(jnp.float32)
    summed = jnp.sum(received, axis=1).transpose(3, 0, 1, 4, 2, 5)
    return summed.reshape(1, CAP, EDGE, width)


def solution(mesh):
    fine = Mesh(mesh.devices.reshape(tuple(SIZES.values())), tuple(SIZES))
    row, col = ("xh", "z"), ("yq", "yb", "xl", "core")
    in_specs = (
        P(None, row, col),
        P(None, col, row),
        P(None, row, col),
        P(None, col, row),
        P(),
    )
    out_specs = P(col, None, None, row)
    return jax.shard_map(body, mesh=fine, in_specs=in_specs, out_specs=out_specs, check_vma=False)
```

```python
import jax
import jax.numpy as jnp
from jax import lax
from jax.experimental import pallas as pl
from jax.experimental.pallas import tpu as pltpu
from jax.sharding import Mesh, PartitionSpec as P

SIZES = {"xh": 2, "z": 12, "yq": 4, "yb": 2, "xl": 2, "core": 2}
GROUP = ("xh", "yb", "xl", "core")
OWNERS = ("xh", "yq", "yb", "xl", "core")
RING = ("xh", "xl")
EDGE = 64
CAP = 3
LANES = 128
PARTS = 16
PART_ROWS = EDGE // PARTS
SLICES = 8
SWAP = [(0, 1), (1, 0)]
GRANT = 24 << 20


def expand(mask, dtype):
    grown = jnp.repeat(jnp.repeat(mask, EDGE, axis=-2), EDGE, axis=-1)
    return grown.astype(dtype)


def turn(value, step):
    return lax.ppermute(value, RING, [(i, (i + step) % 4) for i in range(4)])


def contract(place_ref, select_hbm_ref, left_ref, *rest):
    pieces, (out_ref, select_ref, slab_ref, right_ref, total_ref, sems, select_sem) = rest[:-7], rest[-7:]
    depth = pieces[0].shape[0]
    copies = []
    for number in range(SLICES):
        begin = pl.multiple_of(place_ref[number, 0] * depth, depth)
        started = [
            pltpu.make_async_copy(pieces[2 * number], right_ref.at[2 * number], sems.at[number, 0]),
            pltpu.make_async_copy(
                left_ref.at[:, pl.ds(begin, depth)], slab_ref.at[number], sems.at[number, 1]
            ),
            pltpu.make_async_copy(
                pieces[2 * number + 1], right_ref.at[2 * number + 1], sems.at[number, 2]
            ),
        ]
        for copy in started:
            copy.start()
        copies.append(started)
    select_copy = pltpu.make_async_copy(select_hbm_ref, select_ref, select_sem)
    select_copy.start()
    for number in range(SLICES):
        for copy in copies[number]:
            copy.wait()
        for side in range(2):
            term = jnp.dot(
                slab_ref[number], right_ref[2 * number + side], preferred_element_type=jnp.float32
            )
            half = place_ref[number, 1 + side]
            if number == 0:
                total_ref[half] = term
            else:
                total_ref[half] += term
    select_copy.wait()
    rows = select_ref.shape[0]
    for half in range(2):
        rounded = total_ref[half].astype(jnp.bfloat16)
        stacked = jnp.concatenate([rounded[:, :LANES], rounded[:, LANES:]], axis=0)
        placed = jnp.dot(select_ref[...], stacked, preferred_element_type=jnp.float32)
        out_ref[half * rows:(half + 1) * rows, :] = placed.astype(jnp.bfloat16)


def body(amplitudes, integrals, amp_mask, int_mask, owners):
    panels, rows, depth = amplitudes.shape
    local_tiles = rows // EDGE
    width = integrals.shape[2]
    tile_total = owners.shape[0]
    slot_total = SIZES["yq"] * SLICES * CAP
    xh, yb, xl, core = (lax.axis_index(name) for name in GROUP)

    int_used = integrals * expand(int_mask, integrals.dtype)
    own = int_used.reshape(panels * depth, width)
    across = lax.ppermute(own, "yb", SWAP)
    low = [turn(own, 1), turn(across, 1)]
    high = [turn(own, -1), turn(across, -1)]
    far = [turn(low[0], 1), turn(high[1], -1)]
    here = []
    for near, beyond in (((own, across), far), (low, high)):
        for side in range(2):
            here += [near[side], beyond[side]]
    there = [lax.ppermute(value, "core", SWAP) for value in here]
    chip = xh * 2 + xl
    place = []
    for core_at in (core, 1 - core):
        for first, second in ((0, 2), (3, 1)):
            for side in (yb, 1 - yb):
                one, other = (chip + first) % 4, (chip + second) % 4
                place.append(jnp.stack([side * 4 + (one % 2) * 2 + core_at, one // 2, other // 2]))
    place = jnp.stack(place).astype(jnp.int32)

    amp_used = amplitudes * expand(amp_mask, amplitudes.dtype)
    parts = amp_used.reshape(panels, local_tiles, PARTS, PART_ROWS, depth)
    parts = parts.transpose(2, 0, 1, 3, 4).reshape(PARTS, panels * local_tiles * PART_ROWS, depth)
    traded = lax.all_to_all(parts, GROUP, split_axis=0, concat_axis=0, tiled=True)
    traded = traded.reshape(2, SLICES, panels, local_tiles * PART_ROWS, depth)
    traded = traded.transpose(0, 3, 1, 2, 4).reshape(2 * local_tiles * PART_ROWS, SLICES * panels * depth)
    left = lax.all_gather(traded, "z", axis=0, tiled=True)

    positions = jnp.arange(tile_total, dtype=jnp.int32)
    same_owner = owners[:, None] == owners[None, :]
    earlier = positions[:, None] > positions[None, :]
    slot_index = jnp.sum((same_owner & earlier).astype(jnp.int32), axis=1)
    destination = owners * CAP + slot_index
    order = destination.reshape(2, SIZES["z"], local_tiles).transpose(1, 0, 2).reshape(tile_total)
    source_row = (order[:, None] * PART_ROWS + jnp.arange(PART_ROWS, dtype=jnp.int32)).reshape(-1)
    owner_rows = CAP * PART_ROWS
    source_row = source_row // owner_rows * (2 * owner_rows) + source_row % owner_rows
    source_row = jnp.concatenate([source_row, source_row + owner_rows])
    slot_rows = jnp.arange(2 * slot_total * PART_ROWS, dtype=jnp.int32)
    selector = (slot_rows[:, None] == source_row[None, :]).astype(jnp.bfloat16)

    vmem, anywhere = pl.BlockSpec(memory_space=pltpu.VMEM), pl.BlockSpec(memory_space=pl.ANY)
    held = [pltpu.with_memory_space_constraint(value, pltpu.HBM) for value in [selector, left] + here + there]
    slots = pl.pallas_call(
        contract,
        out_shape=jax.ShapeDtypeStruct((2 * selector.shape[0], LANES), jnp.bfloat16),
        in_specs=[pl.BlockSpec(memory_space=pltpu.SMEM)] + [anywhere] * 18,
        out_specs=vmem,
        scratch_shapes=[
            pltpu.VMEM(selector.shape, jnp.bfloat16),
            pltpu.VMEM((SLICES, left.shape[0], panels * depth), jnp.bfloat16),
            pltpu.VMEM((2 * SLICES, panels * depth, width), jnp.bfloat16),
            pltpu.VMEM((2, left.shape[0], width), jnp.float32),
            pltpu.SemaphoreType.DMA((SLICES, 3)),
            pltpu.SemaphoreType.DMA,
        ],
        compiler_params=pltpu.CompilerParams(vmem_limit_bytes=GRANT),
        cost_estimate=pl.CostEstimate(
            flops=2 * left.size * 2 * width, bytes_accessed=4 * left.size, transcendentals=0
        ),
    )(place, *held)

    received = lax.all_to_all(slots, OWNERS, split_axis=0, concat_axis=0, tiled=True)
    received = received.reshape(2, SIZES["yq"], SLICES, 2, CAP, PART_ROWS, LANES).astype(jnp.float32)
    summed = jnp.sum(received, axis=1).transpose(3, 0, 1, 4, 2, 5)
    return summed.reshape(1, CAP, EDGE, width)


def solution(mesh):
    fine = Mesh(mesh.devices.reshape(tuple(SIZES.values())), tuple(SIZES))
    row, col = ("xh", "z"), ("yq", "yb", "xl", "core")
    in_specs = (
        P(None, row, col),
        P(None, col, row),
        P(None, row, col),
        P(None, col, row),
        P(),
    )
    out_specs = P(col, None, None, row)
    return jax.shard_map(body, mesh=fine, in_specs=in_specs, out_specs=out_specs, check_vma=False)
```

```python
import jax
import jax.numpy as jnp
from jax import lax
from jax.experimental import pallas as pl
from jax.experimental.pallas import tpu as pltpu
from jax.sharding import Mesh, PartitionSpec as P

SIZES = {"xh": 2, "z": 12, "yq": 4, "yb": 2, "xl": 2, "core": 2}
GROUP = ("xh", "yb", "xl", "core")
OWNERS = ("xh", "yq", "yb", "xl", "core")
RING = ("xh", "xl")
EDGE = 64
CAP = 3
LANES = 128
PARTS = 16
PART_ROWS = EDGE // PARTS
TILE_BITS, PART_BITS = EDGE.bit_length() - 1, PART_ROWS.bit_length() - 1
SLICES = 8
SWAP = [(0, 1), (1, 0)]
GRANT = 24 << 20


def expand(mask, dtype):
    grown = jnp.repeat(jnp.repeat(mask, EDGE, axis=-2), EDGE, axis=-1)
    return grown.astype(dtype)


def one_hot(target):
    size = target.shape[1]
    return (lax.broadcasted_iota(jnp.int32, (size, size), 0) == target).astype(jnp.bfloat16)


def masked_parts(mask_hbm_ref, amp_hbm_ref, out_ref, mask_ref, amp_ref, sems):
    copies = [
        pltpu.make_async_copy(mask_hbm_ref, mask_ref, sems.at[0]),
        pltpu.make_async_copy(amp_hbm_ref, amp_ref, sems.at[1]),
    ]
    for copy in copies:
        copy.start()
    panels, rows, depth = amp_ref.shape
    low = lax.broadcasted_iota(jnp.int32, (depth // EDGE, depth), 0) * EDGE
    lane = lax.broadcasted_iota(jnp.int32, (depth // EDGE, depth), 1)
    lane_of = ((lane >= low) & (lane < low + EDGE)).astype(jnp.bfloat16)
    row = lax.broadcasted_iota(jnp.int32, (1, panels * rows), 1)
    block, within = row >> TILE_BITS, row & (EDGE - 1)
    part, inner = within >> PART_BITS, within & (PART_ROWS - 1)
    order = one_hot(part * (panels * rows // PARTS) + block * PART_ROWS + inner)
    for copy in copies:
        copy.wait()
    factors = []
    for tile in range(rows // EDGE):
        mask = mask_ref[tile].astype(jnp.float32).astype(jnp.bfloat16)
        factors.append(jnp.dot(mask, lane_of, preferred_element_type=jnp.float32).astype(jnp.bfloat16))
    blocks = [
        amp_ref[panel, tile * EDGE:(tile + 1) * EDGE, :] * factors[tile][panel:panel + 1]
        for panel in range(panels)
        for tile in range(rows // EDGE)
    ]
    masked = jnp.concatenate(blocks, axis=0)
    out_ref[...] = jnp.dot(order, masked, preferred_element_type=jnp.float32).astype(jnp.bfloat16)


def join(traded_ref, out_ref):
    rows, columns = out_ref.shape
    total, depth = traded_ref.shape
    half, run = total // 2, rows // 2
    row = lax.broadcasted_iota(jnp.int32, (1, total), 1)
    upper = (row >= half).astype(jnp.int32)
    within = row - half * upper
    block = jnp.zeros_like(row)
    for start in range(run, half, run):
        block += (within >= start).astype(jnp.int32)
    order = one_hot(within + run * block + run * upper)
    sorted_rows = jnp.dot(order, traded_ref[...], preferred_element_type=jnp.float32)
    for index in range(columns // depth):
        out_ref[:, index * depth:(index + 1) * depth] = sorted_rows[
            index * rows:(index + 1) * rows
        ].astype(jnp.bfloat16)


def turn(value, step):
    return lax.ppermute(value, RING, [(i, (i + step) % 4) for i in range(4)])


def contract(place_ref, source_ref, left_ref, *rest):
    pieces, (out_ref, slab_ref, right_ref, total_ref, sems) = rest[:-5], rest[-5:]
    depth = pieces[0].shape[0]
    copies = []
    for number in range(SLICES):
        begin = pl.multiple_of(place_ref[number, 0] * depth, depth)
        started = [
            pltpu.make_async_copy(pieces[2 * number], right_ref.at[2 * number], sems.at[number, 0]),
            pltpu.make_async_copy(
                left_ref.at[:, pl.ds(begin, depth)], slab_ref.at[number], sems.at[number, 1]
            ),
            pltpu.make_async_copy(
                pieces[2 * number + 1], right_ref.at[2 * number + 1], sems.at[number, 2]
            ),
        ]
        for copy in started:
            copy.start()
        copies.append(started)
    rows = out_ref.shape[0] // 2
    slot_row = lax.broadcasted_iota(jnp.int32, (rows, source_ref.shape[1]), 0)
    select = (slot_row == source_ref[...]).astype(jnp.bfloat16)
    for number in range(SLICES):
        for copy in copies[number]:
            copy.wait()
        for side in range(2):
            term = jnp.dot(
                slab_ref[number], right_ref[2 * number + side], preferred_element_type=jnp.float32
            )
            half = place_ref[number, 1 + side]
            if number == 0:
                total_ref[half] = term
            else:
                total_ref[half] += term
    for half in range(2):
        rounded = total_ref[half].astype(jnp.bfloat16)
        stacked = jnp.concatenate([rounded[:, :LANES], rounded[:, LANES:]], axis=0)
        placed = jnp.dot(select, stacked, preferred_element_type=jnp.float32)
        out_ref[half * rows:(half + 1) * rows, :] = placed.astype(jnp.bfloat16)


def body(amplitudes, integrals, amp_mask, int_mask, owners):
    panels, rows, depth = amplitudes.shape
    local_tiles = rows // EDGE
    width = integrals.shape[2]
    tile_total = owners.shape[0]
    slot_total = SIZES["yq"] * SLICES * CAP
    xh, yb, xl, core = (lax.axis_index(name) for name in GROUP)

    int_used = integrals * expand(int_mask, integrals.dtype)
    own = int_used.reshape(panels * depth, width)
    across = lax.ppermute(own, "yb", SWAP)
    low = [turn(own, 1), turn(across, 1)]
    high = [turn(own, -1), turn(across, -1)]
    far = [turn(low[0], 1), turn(high[1], -1)]
    here = []
    for near, beyond in (((own, across), far), (low, high)):
        for side in range(2):
            here += [near[side], beyond[side]]
    there = [lax.ppermute(value, "core", SWAP) for value in here]
    chip = xh * 2 + xl
    place = []
    for core_at in (core, 1 - core):
        for first, second in ((0, 2), (3, 1)):
            for side in (yb, 1 - yb):
                one, other = (chip + first) % 4, (chip + second) % 4
                place.append(jnp.stack([side * 4 + (one % 2) * 2 + core_at, one // 2, other // 2]))
    place = jnp.stack(place).astype(jnp.int32)

    vmem, anywhere = pl.BlockSpec(memory_space=pltpu.VMEM), pl.BlockSpec(memory_space=pl.ANY)
    masks = amp_mask.transpose(1, 0, 2)
    parts = pl.pallas_call(
        masked_parts,
        out_shape=jax.ShapeDtypeStruct((panels * rows, depth), jnp.bfloat16),
        in_specs=[anywhere] * 2,
        out_specs=vmem,
        scratch_shapes=[
            pltpu.VMEM(masks.shape, jnp.int32),
            pltpu.VMEM(amplitudes.shape, jnp.bfloat16),
            pltpu.SemaphoreType.DMA((2,)),
        ],
        compiler_params=pltpu.CompilerParams(vmem_limit_bytes=GRANT),
    )(*(pltpu.with_memory_space_constraint(value, pltpu.HBM) for value in (masks, amplitudes)))
    traded = lax.all_to_all(parts, GROUP, split_axis=0, concat_axis=0, tiled=True)
    traded = pl.pallas_call(
        join,
        out_shape=jax.ShapeDtypeStruct((2 * local_tiles * PART_ROWS, SLICES * panels * depth), jnp.bfloat16),
        in_specs=[vmem],
        out_specs=vmem,
        compiler_params=pltpu.CompilerParams(vmem_limit_bytes=GRANT),
    )(traded)
    left = lax.all_gather(traded, "z", axis=0, tiled=True)

    positions = jnp.arange(tile_total, dtype=jnp.int32)
    same_owner = owners[:, None] == owners[None, :]
    earlier = positions[:, None] > positions[None, :]
    slot_index = jnp.sum((same_owner & earlier).astype(jnp.int32), axis=1)
    destination = owners * CAP + slot_index
    order = destination.reshape(2, SIZES["z"], local_tiles).transpose(1, 0, 2).reshape(tile_total)
    source_row = (order[:, None] * PART_ROWS + jnp.arange(PART_ROWS, dtype=jnp.int32)).reshape(-1)
    owner_rows = CAP * PART_ROWS
    source_row = source_row // owner_rows * (2 * owner_rows) + source_row % owner_rows
    source_row = jnp.concatenate([source_row, source_row + owner_rows])

    held = [pltpu.with_memory_space_constraint(value, pltpu.HBM) for value in [left] + here + there]
    slots = pl.pallas_call(
        contract,
        out_shape=jax.ShapeDtypeStruct((4 * slot_total * PART_ROWS, LANES), jnp.bfloat16),
        in_specs=[pl.BlockSpec(memory_space=pltpu.SMEM), vmem] + [anywhere] * 17,
        out_specs=vmem,
        scratch_shapes=[
            pltpu.VMEM((SLICES, left.shape[0], panels * depth), jnp.bfloat16),
            pltpu.VMEM((2 * SLICES, panels * depth, width), jnp.bfloat16),
            pltpu.VMEM((2, left.shape[0], width), jnp.float32),
            pltpu.SemaphoreType.DMA((SLICES, 3)),
        ],
        compiler_params=pltpu.CompilerParams(vmem_limit_bytes=GRANT),
        cost_estimate=pl.CostEstimate(
            flops=2 * left.size * 2 * width, bytes_accessed=4 * left.size, transcendentals=0
        ),
    )(place, source_row[None, :], *held)

    received = lax.all_to_all(slots, OWNERS, split_axis=0, concat_axis=0, tiled=True)
    received = received.reshape(2, SIZES["yq"], SLICES, 2, CAP, PART_ROWS, LANES).astype(jnp.float32)
    summed = jnp.sum(received, axis=1).transpose(3, 0, 1, 4, 2, 5)
    return summed.reshape(1, CAP, EDGE, width)


def solution(mesh):
    fine = Mesh(mesh.devices.reshape(tuple(SIZES.values())), tuple(SIZES))
    row, col = ("xh", "z"), ("yq", "yb", "xl", "core")
    in_specs = (
        P(None, row, col),
        P(None, col, row),
        P(None, row, col),
        P(None, col, row),
        P(),
    )
    out_specs = P(col, None, None, row)
    return jax.shard_map(body, mesh=fine, in_specs=in_specs, out_specs=out_specs, check_vma=False)
```

```python
import jax
import jax.numpy as jnp
from jax import lax
from jax.experimental import pallas as pl
from jax.experimental.pallas import tpu as pltpu
from jax.sharding import Mesh, PartitionSpec as P

SIZES = {"xh": 2, "z": 12, "yq": 4, "yb": 2, "xl": 2, "core": 2}
GROUP = ("xh", "yb", "xl", "core")
OWNERS = ("xh", "yq", "yb", "xl", "core")
RING = ("xh", "xl")
EDGE = 64
CAP = 3
LANES = 128
PARTS = 16
PART_ROWS = EDGE // PARTS
TILE_BITS, PART_BITS = EDGE.bit_length() - 1, PART_ROWS.bit_length() - 1
SLICES = 8
SWAP = [(0, 1), (1, 0)]
GRANT = 24 << 20


def expand(mask, dtype):
    grown = jnp.repeat(jnp.repeat(mask, EDGE, axis=-2), EDGE, axis=-1)
    return grown.astype(dtype)


def one_hot(target):
    size = target.shape[1]
    return (lax.broadcasted_iota(jnp.int32, (size, size), 0) == target).astype(jnp.bfloat16)


def masked_parts(mask_hbm_ref, amp_hbm_ref, out_ref, mask_ref, amp_ref, sems):
    copies = [
        pltpu.make_async_copy(mask_hbm_ref, mask_ref, sems.at[0]),
        pltpu.make_async_copy(amp_hbm_ref, amp_ref, sems.at[1]),
    ]
    for copy in copies:
        copy.start()
    panels, rows, depth = amp_ref.shape
    low = lax.broadcasted_iota(jnp.int32, (depth // EDGE, depth), 0) * EDGE
    lane = lax.broadcasted_iota(jnp.int32, (depth // EDGE, depth), 1)
    lane_of = ((lane >= low) & (lane < low + EDGE)).astype(jnp.bfloat16)
    row = lax.broadcasted_iota(jnp.int32, (1, panels * rows), 1)
    block, within = row >> TILE_BITS, row & (EDGE - 1)
    part, inner = within >> PART_BITS, within & (PART_ROWS - 1)
    order = one_hot(part * (panels * rows // PARTS) + block * PART_ROWS + inner)
    for copy in copies:
        copy.wait()
    factors = []
    for tile in range(rows // EDGE):
        mask = mask_ref[tile].astype(jnp.float32).astype(jnp.bfloat16)
        factors.append(jnp.dot(mask, lane_of, preferred_element_type=jnp.float32).astype(jnp.bfloat16))
    blocks = [
        amp_ref[panel, tile * EDGE:(tile + 1) * EDGE, :] * factors[tile][panel:panel + 1]
        for panel in range(panels)
        for tile in range(rows // EDGE)
    ]
    masked = jnp.concatenate(blocks, axis=0)
    out_ref[...] = jnp.dot(order, masked, preferred_element_type=jnp.float32).astype(jnp.bfloat16)


def join(traded_ref, out_ref):
    rows, columns = out_ref.shape
    total, depth = traded_ref.shape
    half, run = total // 2, rows // 2
    row = lax.broadcasted_iota(jnp.int32, (1, total), 1)
    upper = (row >= half).astype(jnp.int32)
    within = row - half * upper
    block = jnp.zeros_like(row)
    for start in range(run, half, run):
        block += (within >= start).astype(jnp.int32)
    order = one_hot(within + run * block + run * upper)
    sorted_rows = jnp.dot(order, traded_ref[...], preferred_element_type=jnp.float32)
    for index in range(columns // depth):
        out_ref[:, index * depth:(index + 1) * depth] = sorted_rows[
            index * rows:(index + 1) * rows
        ].astype(jnp.bfloat16)


def turn(value, step):
    return lax.ppermute(value, RING, [(i, (i + step) % 4) for i in range(4)])


def contract(place_ref, source_ref, left_ref, *rest):
    pieces, (out_ref, slab_ref, right_ref, total_ref, sems) = rest[:-5], rest[-5:]
    depth = pieces[0].shape[0]
    own = place_ref[0, 1]

    def piece_copy(number, side, half):
        return pltpu.make_async_copy(
            pieces[2 * number + side], right_ref.at[half, number], sems.at[number, half]
        )

    def start_piece(number, half):
        if number % 4 < 2:
            piece_copy(number, half, half).start()
        else:
            first_is_own = place_ref[number, 1] == own

            @pl.when(first_is_own)
            def _():
                piece_copy(number, half, half).start()

            @pl.when(jnp.logical_not(first_is_own))
            def _():
                piece_copy(number, 1 - half, half).start()

    slab_copies = []
    for number in range(SLICES):
        begin = pl.multiple_of(place_ref[number, 0] * depth, depth)
        copy = pltpu.make_async_copy(
            left_ref.at[:, pl.ds(begin, depth)], slab_ref.at[number], sems.at[number, 2]
        )
        copy.start()
        slab_copies.append(copy)
        start_piece(number, 0)
    for number in range(SLICES):
        start_piece(number, 1)
    rows = out_ref.shape[0] // 2
    slot_row = lax.broadcasted_iota(jnp.int32, (rows, source_ref.shape[1]), 0)
    select = (slot_row == source_ref[...]).astype(jnp.bfloat16)
    for half in range(2):
        for number in range(SLICES):
            if half == 0:
                slab_copies[number].wait()
            piece_copy(number, 0, half).wait()
            term = jnp.dot(slab_ref[number], right_ref[half, number], preferred_element_type=jnp.float32)
            if number == 0:
                total_ref[half] = term
            else:
                total_ref[half] += term
        rounded = total_ref[half].astype(jnp.bfloat16)
        stacked = jnp.concatenate([rounded[:, :LANES], rounded[:, LANES:]], axis=0)
        placed = jnp.dot(select, stacked, preferred_element_type=jnp.float32)
        side = own if half == 0 else 1 - own
        begin = pl.multiple_of(side * rows, rows)
        out_ref[pl.ds(begin, rows), :] = placed.astype(jnp.bfloat16)


def body(amplitudes, integrals, amp_mask, int_mask, owners):
    panels, rows, depth = amplitudes.shape
    local_tiles = rows // EDGE
    width = integrals.shape[2]
    tile_total = owners.shape[0]
    slot_total = SIZES["yq"] * SLICES * CAP
    xh, yb, xl, core = (lax.axis_index(name) for name in GROUP)

    int_used = integrals * expand(int_mask, integrals.dtype)
    own = int_used.reshape(panels * depth, width)
    across = lax.ppermute(own, "yb", SWAP)
    low = [turn(own, 1), turn(across, 1)]
    high = [turn(own, -1), turn(across, -1)]
    far = [turn(low[0], 1), turn(high[1], -1)]
    here = []
    for near, beyond in (((own, across), far), (low, high)):
        for side in range(2):
            here += [near[side], beyond[side]]
    there = [lax.ppermute(value, "core", SWAP) for value in here]
    chip = xh * 2 + xl
    place = []
    for core_at in (core, 1 - core):
        for first, second in ((0, 2), (3, 1)):
            for side in (yb, 1 - yb):
                one, other = (chip + first) % 4, (chip + second) % 4
                place.append(jnp.stack([side * 4 + (one % 2) * 2 + core_at, one // 2, other // 2]))
    place = jnp.stack(place).astype(jnp.int32)

    vmem, anywhere = pl.BlockSpec(memory_space=pltpu.VMEM), pl.BlockSpec(memory_space=pl.ANY)
    masks = amp_mask.transpose(1, 0, 2)
    parts = pl.pallas_call(
        masked_parts,
        out_shape=jax.ShapeDtypeStruct((panels * rows, depth), jnp.bfloat16),
        in_specs=[anywhere] * 2,
        out_specs=vmem,
        scratch_shapes=[
            pltpu.VMEM(masks.shape, jnp.int32),
            pltpu.VMEM(amplitudes.shape, jnp.bfloat16),
            pltpu.SemaphoreType.DMA((2,)),
        ],
        compiler_params=pltpu.CompilerParams(vmem_limit_bytes=GRANT),
    )(*(pltpu.with_memory_space_constraint(value, pltpu.HBM) for value in (masks, amplitudes)))
    traded = lax.all_to_all(parts, GROUP, split_axis=0, concat_axis=0, tiled=True)
    traded = pl.pallas_call(
        join,
        out_shape=jax.ShapeDtypeStruct((2 * local_tiles * PART_ROWS, SLICES * panels * depth), jnp.bfloat16),
        in_specs=[vmem],
        out_specs=vmem,
        compiler_params=pltpu.CompilerParams(vmem_limit_bytes=GRANT),
    )(traded)
    left = lax.all_gather(traded, "z", axis=0, tiled=True)

    positions = jnp.arange(tile_total, dtype=jnp.int32)
    same_owner = owners[:, None] == owners[None, :]
    earlier = positions[:, None] > positions[None, :]
    slot_index = jnp.sum((same_owner & earlier).astype(jnp.int32), axis=1)
    destination = owners * CAP + slot_index
    order = destination.reshape(2, SIZES["z"], local_tiles).transpose(1, 0, 2).reshape(tile_total)
    source_row = (order[:, None] * PART_ROWS + jnp.arange(PART_ROWS, dtype=jnp.int32)).reshape(-1)
    owner_rows = CAP * PART_ROWS
    source_row = source_row // owner_rows * (2 * owner_rows) + source_row % owner_rows
    source_row = jnp.concatenate([source_row, source_row + owner_rows])

    held = [pltpu.with_memory_space_constraint(value, pltpu.HBM) for value in [left] + here + there]
    slots = pl.pallas_call(
        contract,
        out_shape=jax.ShapeDtypeStruct((4 * slot_total * PART_ROWS, LANES), jnp.bfloat16),
        in_specs=[pl.BlockSpec(memory_space=pltpu.SMEM), vmem] + [anywhere] * 17,
        out_specs=vmem,
        scratch_shapes=[
            pltpu.VMEM((SLICES, left.shape[0], panels * depth), jnp.bfloat16),
            pltpu.VMEM((2, SLICES, panels * depth, width), jnp.bfloat16),
            pltpu.VMEM((2, left.shape[0], width), jnp.float32),
            pltpu.SemaphoreType.DMA((SLICES, 3)),
        ],
        compiler_params=pltpu.CompilerParams(vmem_limit_bytes=GRANT),
        cost_estimate=pl.CostEstimate(
            flops=2 * left.size * 2 * width, bytes_accessed=4 * left.size, transcendentals=0
        ),
    )(place, source_row[None, :], *held)

    received = lax.all_to_all(slots, OWNERS, split_axis=0, concat_axis=0, tiled=True)
    received = received.reshape(2, SIZES["yq"], SLICES, 2, CAP, PART_ROWS, LANES).astype(jnp.float32)
    summed = jnp.sum(received, axis=1).transpose(3, 0, 1, 4, 2, 5)
    return summed.reshape(1, CAP, EDGE, width)


def solution(mesh):
    fine = Mesh(mesh.devices.reshape(tuple(SIZES.values())), tuple(SIZES))
    row, col = ("xh", "z"), ("yq", "yb", "xl", "core")
    in_specs = (
        P(None, row, col),
        P(None, col, row),
        P(None, row, col),
        P(None, col, row),
        P(),
    )
    out_specs = P(col, None, None, row)
    return jax.shard_map(body, mesh=fine, in_specs=in_specs, out_specs=out_specs, check_vma=False)
```

```python
import jax
import jax.numpy as jnp
from jax import lax
from jax.experimental import pallas as pl
from jax.experimental.pallas import tpu as pltpu
from jax.sharding import Mesh, PartitionSpec as P

SIZES = {"xh": 2, "z": 12, "yq": 4, "yb": 2, "xl": 2, "core": 2}
GROUP = ("xh", "yb", "xl", "core")
OWNERS = ("xh", "yq", "yb", "xl", "core")
RING = ("xh", "xl")
EDGE = 64
CAP = 3
LANES = 128
PARTS = 16
PART_ROWS = EDGE // PARTS
TILE_BITS, PART_BITS = EDGE.bit_length() - 1, PART_ROWS.bit_length() - 1
SLICES = 8
SWAP = [(0, 1), (1, 0)]
GRANT = 24 << 20


def expand(mask, dtype):
    grown = jnp.repeat(jnp.repeat(mask, EDGE, axis=-2), EDGE, axis=-1)
    return grown.astype(dtype)


def one_hot(target):
    size = target.shape[1]
    return (lax.broadcasted_iota(jnp.int32, (size, size), 0) == target).astype(jnp.bfloat16)


def masked_parts(mask_hbm_ref, amp_hbm_ref, out_ref, mask_ref, amp_ref, sems):
    copies = [
        pltpu.make_async_copy(mask_hbm_ref, mask_ref, sems.at[0]),
        pltpu.make_async_copy(amp_hbm_ref, amp_ref, sems.at[1]),
    ]
    for copy in copies:
        copy.start()
    panels, rows, depth = amp_ref.shape
    low = lax.broadcasted_iota(jnp.int32, (depth // EDGE, depth), 0) * EDGE
    lane = lax.broadcasted_iota(jnp.int32, (depth // EDGE, depth), 1)
    lane_of = ((lane >= low) & (lane < low + EDGE)).astype(jnp.bfloat16)
    row = lax.broadcasted_iota(jnp.int32, (1, panels * rows), 1)
    block, within = row >> TILE_BITS, row & (EDGE - 1)
    part, inner = within >> PART_BITS, within & (PART_ROWS - 1)
    order = one_hot(part * (panels * rows // PARTS) + block * PART_ROWS + inner)
    for copy in copies:
        copy.wait()
    factors = []
    for tile in range(rows // EDGE):
        mask = mask_ref[tile].astype(jnp.float32).astype(jnp.bfloat16)
        factors.append(jnp.dot(mask, lane_of, preferred_element_type=jnp.float32).astype(jnp.bfloat16))
    blocks = [
        amp_ref[panel, tile * EDGE:(tile + 1) * EDGE, :] * factors[tile][panel:panel + 1]
        for panel in range(panels)
        for tile in range(rows // EDGE)
    ]
    masked = jnp.concatenate(blocks, axis=0)
    out_ref[...] = jnp.dot(order, masked, preferred_element_type=jnp.float32).astype(jnp.bfloat16)


def join(traded_ref, out_ref):
    rows, columns = out_ref.shape
    total, depth = traded_ref.shape
    half, run = total // 2, rows // 2
    row = lax.broadcasted_iota(jnp.int32, (1, total), 1)
    upper = (row >= half).astype(jnp.int32)
    within = row - half * upper
    block = jnp.zeros_like(row)
    for start in range(run, half, run):
        block += (within >= start).astype(jnp.int32)
    order = one_hot(within + run * block + run * upper)
    sorted_rows = jnp.dot(order, traded_ref[...], preferred_element_type=jnp.float32)
    for index in range(columns // depth):
        out_ref[:, index * depth:(index + 1) * depth] = sorted_rows[
            index * rows:(index + 1) * rows
        ].astype(jnp.bfloat16)


def turn(value, step):
    return lax.ppermute(value, RING, [(i, (i + step) % 4) for i in range(4)])


def contract(place_ref, source_ref, left_ref, *rest):
    pieces, (out_ref, slab_ref, right_ref, total_ref, sems) = rest[:-5], rest[-5:]
    depth = pieces[0].shape[0]
    copies = []
    for number in range(SLICES):
        begin = pl.multiple_of(place_ref[number, 0] * depth, depth)
        started = [
            pltpu.make_async_copy(pieces[2 * number], right_ref.at[2 * number], sems.at[number, 0]),
            pltpu.make_async_copy(
                left_ref.at[:, pl.ds(begin, depth)], slab_ref.at[number], sems.at[number, 1]
            ),
            pltpu.make_async_copy(
                pieces[2 * number + 1], right_ref.at[2 * number + 1], sems.at[number, 2]
            ),
        ]
        for copy in started:
            copy.start()
        copies.append(started)
    rows = out_ref.shape[0] // 2
    tile_rows = source_ref.shape[1]
    run = CAP * PART_ROWS
    inverse = -(-(1 << 16) // (2 * run))

    def second_block(lanes):
        row = lax.broadcasted_iota(jnp.int32, (rows, lanes), 0)
        return row, row - ((row * inverse) >> 16) * (2 * run) >= run

    row, second = second_block(tile_rows)
    select = (jnp.where(second, row - run, row) == source_ref[...]).astype(jnp.bfloat16)
    _, second = second_block(LANES)
    for number in range(SLICES):
        for copy in copies[number]:
            copy.wait()
        for side in range(2):
            term = jnp.dot(
                slab_ref[number], right_ref[2 * number + side], preferred_element_type=jnp.float32
            )
            half = place_ref[number, 1 + side]
            if number == 0:
                total_ref[half] = term
            else:
                total_ref[half] += term
    for half in range(2):
        rounded = total_ref[half].astype(jnp.bfloat16)
        placed = jnp.dot(select, rounded, preferred_element_type=jnp.float32)
        placed = jnp.where(second, placed[:, LANES:], placed[:, :LANES])
        out_ref[half * rows:(half + 1) * rows, :] = placed.astype(jnp.bfloat16)


def body(amplitudes, integrals, amp_mask, int_mask, owners):
    panels, rows, depth = amplitudes.shape
    local_tiles = rows // EDGE
    width = integrals.shape[2]
    tile_total = owners.shape[0]
    slot_total = SIZES["yq"] * SLICES * CAP
    xh, yb, xl, core = (lax.axis_index(name) for name in GROUP)

    int_used = integrals * expand(int_mask, integrals.dtype)
    own = int_used.reshape(panels * depth, width)
    across = lax.ppermute(own, "yb", SWAP)
    low = [turn(own, 1), turn(across, 1)]
    high = [turn(own, -1), turn(across, -1)]
    far = [turn(low[0], 1), turn(high[1], -1)]
    here = []
    for near, beyond in (((own, across), far), (low, high)):
        for side in range(2):
            here += [near[side], beyond[side]]
    there = [lax.ppermute(value, "core", SWAP) for value in here]
    chip = xh * 2 + xl
    place = []
    for core_at in (core, 1 - core):
        for first, second in ((0, 2), (3, 1)):
            for side in (yb, 1 - yb):
                one, other = (chip + first) % 4, (chip + second) % 4
                place.append(jnp.stack([side * 4 + (one % 2) * 2 + core_at, one // 2, other // 2]))
    place = jnp.stack(place).astype(jnp.int32)

    vmem, anywhere = pl.BlockSpec(memory_space=pltpu.VMEM), pl.BlockSpec(memory_space=pl.ANY)
    masks = amp_mask.transpose(1, 0, 2)
    parts = pl.pallas_call(
        masked_parts,
        out_shape=jax.ShapeDtypeStruct((panels * rows, depth), jnp.bfloat16),
        in_specs=[anywhere] * 2,
        out_specs=vmem,
        scratch_shapes=[
            pltpu.VMEM(masks.shape, jnp.int32),
            pltpu.VMEM(amplitudes.shape, jnp.bfloat16),
            pltpu.SemaphoreType.DMA((2,)),
        ],
        compiler_params=pltpu.CompilerParams(vmem_limit_bytes=GRANT),
    )(*(pltpu.with_memory_space_constraint(value, pltpu.HBM) for value in (masks, amplitudes)))
    traded = lax.all_to_all(parts, GROUP, split_axis=0, concat_axis=0, tiled=True)
    traded = pl.pallas_call(
        join,
        out_shape=jax.ShapeDtypeStruct((2 * local_tiles * PART_ROWS, SLICES * panels * depth), jnp.bfloat16),
        in_specs=[vmem],
        out_specs=vmem,
        compiler_params=pltpu.CompilerParams(vmem_limit_bytes=GRANT),
    )(traded)
    left = lax.all_gather(traded, "z", axis=0, tiled=True)

    positions = jnp.arange(tile_total, dtype=jnp.int32)
    same_owner = owners[:, None] == owners[None, :]
    earlier = positions[:, None] > positions[None, :]
    slot_index = jnp.sum((same_owner & earlier).astype(jnp.int32), axis=1)
    destination = owners * CAP + slot_index
    order = destination.reshape(2, SIZES["z"], local_tiles).transpose(1, 0, 2).reshape(tile_total)
    source_row = (order[:, None] * PART_ROWS + jnp.arange(PART_ROWS, dtype=jnp.int32)).reshape(-1)
    owner_rows = CAP * PART_ROWS
    source_row = source_row // owner_rows * (2 * owner_rows) + source_row % owner_rows

    held = [pltpu.with_memory_space_constraint(value, pltpu.HBM) for value in [left] + here + there]
    slots = pl.pallas_call(
        contract,
        out_shape=jax.ShapeDtypeStruct((4 * slot_total * PART_ROWS, LANES), jnp.bfloat16),
        in_specs=[pl.BlockSpec(memory_space=pltpu.SMEM), vmem] + [anywhere] * 17,
        out_specs=vmem,
        scratch_shapes=[
            pltpu.VMEM((SLICES, left.shape[0], panels * depth), jnp.bfloat16),
            pltpu.VMEM((2 * SLICES, panels * depth, width), jnp.bfloat16),
            pltpu.VMEM((2, left.shape[0], width), jnp.float32),
            pltpu.SemaphoreType.DMA((SLICES, 3)),
        ],
        compiler_params=pltpu.CompilerParams(vmem_limit_bytes=GRANT),
        cost_estimate=pl.CostEstimate(
            flops=2 * left.size * 2 * width, bytes_accessed=4 * left.size, transcendentals=0
        ),
    )(place, source_row[None, :], *held)

    received = lax.all_to_all(slots, OWNERS, split_axis=0, concat_axis=0, tiled=True)
    received = received.reshape(2, SIZES["yq"], SLICES, 2, CAP, PART_ROWS, LANES).astype(jnp.float32)
    summed = jnp.sum(received, axis=1).transpose(3, 0, 1, 4, 2, 5)
    return summed.reshape(1, CAP, EDGE, width)


def solution(mesh):
    fine = Mesh(mesh.devices.reshape(tuple(SIZES.values())), tuple(SIZES))
    row, col = ("xh", "z"), ("yq", "yb", "xl", "core")
    in_specs = (
        P(None, row, col),
        P(None, col, row),
        P(None, row, col),
        P(None, col, row),
        P(),
    )
    out_specs = P(col, None, None, row)
    return jax.shard_map(body, mesh=fine, in_specs=in_specs, out_specs=out_specs, check_vma=False)
```

```python
import jax
import jax.numpy as jnp
from jax import lax
from jax.experimental import pallas as pl
from jax.experimental.pallas import tpu as pltpu
from jax.sharding import Mesh, PartitionSpec as P

SIZES = {"xh": 2, "z": 12, "yq": 4, "yb": 2, "xl": 2, "core": 2}
GROUP = ("xh", "yb", "xl", "core")
OWNERS = ("xh", "yq", "yb", "xl", "core")
RING = ("xh", "xl")
EDGE = 64
CAP = 3
LANES = 128
PARTS = 16
PART_ROWS = EDGE // PARTS
TILE_BITS, PART_BITS = EDGE.bit_length() - 1, PART_ROWS.bit_length() - 1
SLICES = 8
SWAP = [(0, 1), (1, 0)]
GRANT = 24 << 20


def expand(mask, dtype):
    grown = jnp.repeat(jnp.repeat(mask, EDGE, axis=-2), EDGE, axis=-1)
    return grown.astype(dtype)


def one_hot(target):
    size = target.shape[1]
    return (lax.broadcasted_iota(jnp.int32, (size, size), 0) == target).astype(jnp.bfloat16)


def masked_parts(mask_hbm_ref, amp_hbm_ref, out_ref, mask_ref, amp_ref, sems):
    copies = [
        pltpu.make_async_copy(mask_hbm_ref, mask_ref, sems.at[0]),
        pltpu.make_async_copy(amp_hbm_ref, amp_ref, sems.at[1]),
    ]
    for copy in copies:
        copy.start()
    panels, rows, depth = amp_ref.shape
    low = lax.broadcasted_iota(jnp.int32, (depth // EDGE, depth), 0) * EDGE
    lane = lax.broadcasted_iota(jnp.int32, (depth // EDGE, depth), 1)
    lane_of = ((lane >= low) & (lane < low + EDGE)).astype(jnp.bfloat16)
    row = lax.broadcasted_iota(jnp.int32, (1, panels * rows), 1)
    block, within = row >> TILE_BITS, row & (EDGE - 1)
    part, inner = within >> PART_BITS, within & (PART_ROWS - 1)
    order = one_hot(part * (panels * rows // PARTS) + block * PART_ROWS + inner)
    for copy in copies:
        copy.wait()
    factors = []
    for tile in range(rows // EDGE):
        mask = mask_ref[tile].astype(jnp.float32).astype(jnp.bfloat16)
        factors.append(jnp.dot(mask, lane_of, preferred_element_type=jnp.float32).astype(jnp.bfloat16))
    blocks = [
        amp_ref[panel, tile * EDGE:(tile + 1) * EDGE, :] * factors[tile][panel:panel + 1]
        for panel in range(panels)
        for tile in range(rows // EDGE)
    ]
    masked = jnp.concatenate(blocks, axis=0)
    out_ref[...] = jnp.dot(order, masked, preferred_element_type=jnp.float32).astype(jnp.bfloat16)


def join(traded_ref, out_ref):
    rows, columns = out_ref.shape
    total, depth = traded_ref.shape
    half, run = total // 2, rows // 2
    row = lax.broadcasted_iota(jnp.int32, (1, total), 1)
    upper = (row >= half).astype(jnp.int32)
    within = row - half * upper
    block = jnp.zeros_like(row)
    for start in range(run, half, run):
        block += (within >= start).astype(jnp.int32)
    order = one_hot(within + run * block + run * upper)
    sorted_rows = jnp.dot(order, traded_ref[...], preferred_element_type=jnp.float32)
    for index in range(columns // depth):
        out_ref[:, index * depth:(index + 1) * depth] = sorted_rows[
            index * rows:(index + 1) * rows
        ].astype(jnp.bfloat16)


def turn(value, step):
    return lax.ppermute(value, RING, [(i, (i + step) % 4) for i in range(4)])


def contract(place_ref, source_ref, left_ref, *rest):
    pieces, (out_ref, slab_ref, right_ref, total_ref, sems) = rest[:-5], rest[-5:]
    depth, width = pieces[0].shape
    copies = []
    for number in range(SLICES):
        begin = pl.multiple_of(place_ref[number, 0] * depth, depth)
        started = [
            pltpu.make_async_copy(
                left_ref.at[:, pl.ds(begin, depth)], slab_ref.at[number], sems.at[number, 2]
            )
        ]
        for side in range(2):
            lane = pl.multiple_of(place_ref[number, 1 + side] * width, width)
            started.append(pltpu.make_async_copy(
                pieces[2 * number + side], right_ref.at[number, :, pl.ds(lane, width)], sems.at[number, side]
            ))
        for copy in started:
            copy.start()
        copies.append(started)
    rows = out_ref.shape[0] // 2
    tile_rows = source_ref.shape[1]
    run = CAP * PART_ROWS
    inverse = -(-(1 << 16) // (2 * run))

    def second_block(lanes):
        row = lax.broadcasted_iota(jnp.int32, (rows, lanes), 0)
        return row, row - ((row * inverse) >> 16) * (2 * run) >= run

    row, second = second_block(tile_rows)
    select = (jnp.where(second, row - run, row) == source_ref[...]).astype(jnp.bfloat16)
    _, second = second_block(LANES)
    for number in range(SLICES):
        for copy in copies[number]:
            copy.wait()
        term = jnp.dot(slab_ref[number], right_ref[number], preferred_element_type=jnp.float32)
        if number == 0:
            total_ref[...] = term
        else:
            total_ref[...] += term
    for half in range(2):
        rounded = total_ref[:, half * width:(half + 1) * width].astype(jnp.bfloat16)
        placed = jnp.dot(select, rounded, preferred_element_type=jnp.float32)
        placed = jnp.where(second, placed[:, LANES:], placed[:, :LANES])
        out_ref[half * rows:(half + 1) * rows, :] = placed.astype(jnp.bfloat16)


def body(amplitudes, integrals, amp_mask, int_mask, owners):
    panels, rows, depth = amplitudes.shape
    local_tiles = rows // EDGE
    width = integrals.shape[2]
    tile_total = owners.shape[0]
    slot_total = SIZES["yq"] * SLICES * CAP
    xh, yb, xl, core = (lax.axis_index(name) for name in GROUP)

    int_used = integrals * expand(int_mask, integrals.dtype)
    own = int_used.reshape(panels * depth, width)
    across = lax.ppermute(own, "yb", SWAP)
    low = [turn(own, 1), turn(across, 1)]
    high = [turn(own, -1), turn(across, -1)]
    far = [turn(low[0], 1), turn(high[1], -1)]
    here = []
    for near, beyond in (((own, across), far), (low, high)):
        for side in range(2):
            here += [near[side], beyond[side]]
    there = [lax.ppermute(value, "core", SWAP) for value in here]
    chip = xh * 2 + xl
    place = []
    for core_at in (core, 1 - core):
        for first, second in ((0, 2), (3, 1)):
            for side in (yb, 1 - yb):
                one, other = (chip + first) % 4, (chip + second) % 4
                place.append(jnp.stack([side * 4 + (one % 2) * 2 + core_at, one // 2, other // 2]))
    place = jnp.stack(place).astype(jnp.int32)

    vmem, anywhere = pl.BlockSpec(memory_space=pltpu.VMEM), pl.BlockSpec(memory_space=pl.ANY)
    masks = amp_mask.transpose(1, 0, 2)
    parts = pl.pallas_call(
        masked_parts,
        out_shape=jax.ShapeDtypeStruct((panels * rows, depth), jnp.bfloat16),
        in_specs=[anywhere] * 2,
        out_specs=vmem,
        scratch_shapes=[
            pltpu.VMEM(masks.shape, jnp.int32),
            pltpu.VMEM(amplitudes.shape, jnp.bfloat16),
            pltpu.SemaphoreType.DMA((2,)),
        ],
        compiler_params=pltpu.CompilerParams(vmem_limit_bytes=GRANT),
    )(*(pltpu.with_memory_space_constraint(value, pltpu.HBM) for value in (masks, amplitudes)))
    traded = lax.all_to_all(parts, GROUP, split_axis=0, concat_axis=0, tiled=True)
    traded = pl.pallas_call(
        join,
        out_shape=jax.ShapeDtypeStruct((2 * local_tiles * PART_ROWS, SLICES * panels * depth), jnp.bfloat16),
        in_specs=[vmem],
        out_specs=vmem,
        compiler_params=pltpu.CompilerParams(vmem_limit_bytes=GRANT),
    )(traded)
    left = lax.all_gather(traded, "z", axis=0, tiled=True)

    positions = jnp.arange(tile_total, dtype=jnp.int32)
    same_owner = owners[:, None] == owners[None, :]
    earlier = positions[:, None] > positions[None, :]
    slot_index = jnp.sum((same_owner & earlier).astype(jnp.int32), axis=1)
    destination = owners * CAP + slot_index
    order = destination.reshape(2, SIZES["z"], local_tiles).transpose(1, 0, 2).reshape(tile_total)
    source_row = (order[:, None] * PART_ROWS + jnp.arange(PART_ROWS, dtype=jnp.int32)).reshape(-1)
    owner_rows = CAP * PART_ROWS
    source_row = source_row // owner_rows * (2 * owner_rows) + source_row % owner_rows

    held = [pltpu.with_memory_space_constraint(value, pltpu.HBM) for value in [left] + here + there]
    slots = pl.pallas_call(
        contract,
        out_shape=jax.ShapeDtypeStruct((4 * slot_total * PART_ROWS, LANES), jnp.bfloat16),
        in_specs=[pl.BlockSpec(memory_space=pltpu.SMEM), vmem] + [anywhere] * 17,
        out_specs=vmem,
        scratch_shapes=[
            pltpu.VMEM((SLICES, left.shape[0], panels * depth), jnp.bfloat16),
            pltpu.VMEM((SLICES, panels * depth, 2 * width), jnp.bfloat16),
            pltpu.VMEM((left.shape[0], 2 * width), jnp.float32),
            pltpu.SemaphoreType.DMA((SLICES, 3)),
        ],
        compiler_params=pltpu.CompilerParams(vmem_limit_bytes=GRANT),
        cost_estimate=pl.CostEstimate(
            flops=2 * left.size * 2 * width, bytes_accessed=4 * left.size, transcendentals=0
        ),
    )(place, source_row[None, :], *held)

    received = lax.all_to_all(slots, OWNERS, split_axis=0, concat_axis=0, tiled=True)
    received = received.reshape(2, SIZES["yq"], SLICES, 2, CAP, PART_ROWS, LANES).astype(jnp.float32)
    summed = jnp.sum(received, axis=1).transpose(3, 0, 1, 4, 2, 5)
    return summed.reshape(1, CAP, EDGE, width)


def solution(mesh):
    fine = Mesh(mesh.devices.reshape(tuple(SIZES.values())), tuple(SIZES))
    row, col = ("xh", "z"), ("yq", "yb", "xl", "core")
    in_specs = (
        P(None, row, col),
        P(None, col, row),
        P(None, row, col),
        P(None, col, row),
        P(),
    )
    out_specs = P(col, None, None, row)
    return jax.shard_map(body, mesh=fine, in_specs=in_specs, out_specs=out_specs, check_vma=False)
```
